32 devices in a mesh: dp: 8 (over y, x, core), seq: 4 (over z).
Axes of the slice: x: 2, y: 2, z: 4, core: 2. Of those that a mesh axis runs over, the one named last changes fastest.
Arguments:
- image_query: bfloat16 [8, 256, 1536], P('dp', 'seq'), may hold values from -300 to 300
- image_key: bfloat16 [8, 256, 1536], P('dp', 'seq'), may hold values from -300 to 300
- image_value: bfloat16 [8, 256, 1536], P('dp', 'seq'), may hold values from -6 to 6
- text_key: bfloat16 [8, 512, 1536], P('dp', 'seq'), may hold values from -300 to 300
- text_value: bfloat16 [8, 512, 1536], P('dp', 'seq'), may hold values from -6 to 6
- query_gain: float32 [128], replicated, may hold values from 0.6 to 1.8
- key_gain: float32 [128], replicated, may hold values from 0.6 to 1.8
- embed_weight: bfloat16 [1536, 1408], replicated, may hold values from -0.15625 to 0.15625
- position_embed: float32 [64, 1408], replicated, may hold values from -2.7 to 2.7
- norm_gain: float32 [1408], replicated, may hold values from 0.25 to 1.75
- final_gain: float32 [1408], replicated, may hold values from 0.25 to 1.75
- up_weight: bfloat16 [3072, 1408], P(('dp', 'seq')), may hold values from -0.15625 to 0.15625
- down_weight: bfloat16 [3072, 1408], P(('dp', 'seq')), may hold values from -0.109375 to 0.109375
- reward_direction: float32 [1408], replicated, may hold values from -1.5 to 1.5
Outputs:
- attended: bfloat16 [8, 256, 1536], P('dp', None, 'seq')
- attended_gradient: bfloat16 [8, 256, 1536], P('dp', None, 'seq')
- reward: float32 [8], P('dp')
The draws below stay inside these ranges and needn't reach their ends.
All inputs are finite; a program needn't handle non-finite values.
Results may differ from the reference program's by a relative error of at most 0.02.
Values may be sent and summed in bfloat16 or wider, within the bound.
A program may use at most 64 MiB of HBM per device.

```python
import math
import jax
import jax.numpy as jnp
from jax import lax

HEAD = 128
HEADS = 12
HD = 1536
EMB = 1408
HID = 3072
PATCH_W = 32
BATCH = 8
IMG_TOK = 256
TXT_TOK = 512
REW_TOK = 64
N_DP = 8
N_SEQ = 4


def scaled_block(key, array_shape, base_entries, row_range, column_range):
    row_key, column_key = jax.random.split(key)
    row_shape = array_shape[:-1] + (1,)
    row_scale = jnp.exp(jax.random.uniform(row_key, row_shape, jnp.float32, math.log(row_range[0]), math.log(row_range[1])))
    column_scale = jnp.exp(jax.random.uniform(column_key, (array_shape[-1],), jnp.float32, math.log(column_range[0]), math.log(column_range[1])))
    return base_entries * row_scale * column_scale


def projected_draw(key, array_shape):
    entry_key, scale_key = jax.random.split(key)
    base_entries = jax.random.truncated_normal(entry_key, -3.0, 3.0, array_shape, jnp.float32)
    return scaled_block(scale_key, array_shape, base_entries, (1.0, 10.0), (1.0, 10.0))


def draw_image_query(key, part):
    return projected_draw(jax.random.fold_in(key, 11), (BATCH, IMG_TOK, HD)).astype(jnp.bfloat16)


def draw_image_key(key, part):
    return projected_draw(jax.random.fold_in(key, 12), (BATCH, IMG_TOK, HD)).astype(jnp.bfloat16)


def draw_text_key(key, part):
    return projected_draw(jax.random.fold_in(key, 13), (BATCH, TXT_TOK, HD)).astype(jnp.bfloat16)


def draw_position_embed(key, part):
    entry_key, scale_key = jax.random.split(jax.random.fold_in(key, 14))
    array_shape = (REW_TOK, EMB)
    base_entries = jax.random.truncated_normal(entry_key, -3.0, 3.0, array_shape, jnp.float32)
    return scaled_block(scale_key, array_shape, base_entries, (0.03, 0.3), (0.3, 3.0))


def level_of(key, shape, pieces, least, top_value):
    factor_of, own = 1.0, jax.random.fold_in(key, 6)
    for position, parts in pieces:
        draws = jnp.exp(jax.random.uniform(jax.random.fold_in(own, position), (parts,), jnp.float32, least / len(pieces), top_value / len(pieces)))
        factor_of = factor_of * jnp.repeat(draws, shape[position] // parts).reshape([-1 if axis == position else 1 for axis in range(len(shape))])
    return factor_of


def noise(own_key, shape, width, bound, shards=(), held_as=jnp.bfloat16):
    factor_of = level_of(own_key, shape, shards, -0.22, 0.18) if shards else 1.0
    values = jax.random.normal(own_key, shape, jnp.float32) * width * factor_of
    return jnp.minimum(jnp.maximum(values, -bound), bound).astype(held_as)


def setup_inputs(seed: int = 0) -> dict:
    key_of = jax.random.split(jax.random.key(seed), 15)
    image_query = draw_image_query(jax.random.fold_in(key_of[14], 71), 0)
    image_key = draw_image_key(jax.random.fold_in(key_of[14], 71), 0)
    image_value = noise(key_of[2], (BATCH, IMG_TOK, HD), 1.0, 6.0, ((0, 8), (1, 4)))
    text_key = draw_text_key(jax.random.fold_in(key_of[14], 71), 0)
    text_value = noise(key_of[4], (BATCH, TXT_TOK, HD), 1.0, 6.0, ((0, 8), (1, 4)))
    query_gain = jnp.clip(jax.random.uniform(key_of[5], (HEAD,), jnp.float32, 0.6, 1.8), 0.6, 1.8)
    key_gain = jnp.clip(jax.random.uniform(key_of[6], (HEAD,), jnp.float32, 0.6, 1.8), 0.6, 1.8)
    embed_weight = noise(key_of[7], (HD, EMB), HD ** -0.5, 0.15625)
    position_embed = draw_position_embed(jax.random.fold_in(key_of[14], 71), 0)
    norm_gain = jnp.clip(1.0 + 0.15 * jax.random.normal(key_of[9], (EMB,), jnp.float32), 0.25, 1.75)
    final_gain = jnp.clip(1.0 + 0.15 * jax.random.normal(key_of[10], (EMB,), jnp.float32), 0.25, 1.75)
    up_weight = noise(key_of[11], (HID, EMB), EMB ** -0.5, 0.15625, ((0, 32),))
    down_weight = noise(key_of[12], (HID, EMB), HID ** -0.5, 0.109375, ((0, 32),))
    reward_direction = noise(key_of[13], (EMB,), 0.25, 1.5, (), jnp.float32)
    return dict(image_query=image_query, image_key=image_key, image_value=image_value, text_key=text_key, text_value=text_value, query_gain=query_gain, key_gain=key_gain, embed_weight=embed_weight, position_embed=position_embed, norm_gain=norm_gain, final_gain=final_gain, up_weight=up_weight, down_weight=down_weight, reward_direction=reward_direction)


epsilon = 1e-06
root_half = 0.7071067811865476
inv_root_tau = 0.3989422804014327

def norm_heads(features, gain_vector):
    token_count = features.shape[0]
    grouped = features.astype(jnp.float32).reshape(token_count, -1, HEAD)
    inverse_rms = lax.rsqrt(lax.optimization_barrier(jnp.mean(grouped * grouped, axis=-1, keepdims=True)) + epsilon)
    return (grouped * inverse_rms * gain_vector).astype(jnp.bfloat16)

def layer_stats(residual):
    centered = residual - lax.optimization_barrier(jnp.mean(residual, axis=-1, keepdims=True))
    inverse_std = lax.rsqrt(lax.optimization_barrier(jnp.mean(centered * centered, axis=-1, keepdims=True)) + epsilon)
    return (centered * inverse_std, inverse_std)

def layer_back(upstream, normed, inverse_std):
    return inverse_std * (upstream - lax.optimization_barrier(jnp.mean(upstream, axis=-1, keepdims=True)) - normed * lax.optimization_barrier(jnp.mean(upstream * normed, axis=-1, keepdims=True)))

def gelu_parts(preact):
    cumulative = 0.5 * (1.0 + lax.erf(preact * root_half))
    activation = preact * cumulative
    derivative = cumulative + preact * jnp.exp(-0.5 * preact * preact) * inv_root_tau
    return (activation, derivative)

def pool_patches(attended):
    token_count, feature_width = attended.shape
    patch_grid = attended.astype(jnp.float32).reshape(token_count // PATCH_W // 2, 2, PATCH_W // 2, 2, feature_width)
    return lax.optimization_barrier(jnp.mean(patch_grid, axis=(1, 3))).reshape(-1, feature_width).astype(jnp.bfloat16)

def spread_patches(pooled_slope):
    pooled_count, feature_width = pooled_slope.shape
    row_count = pooled_count // (PATCH_W // 2)
    patch_grid = pooled_slope.reshape(row_count, 1, PATCH_W // 2, 1, feature_width)
    patch_grid = jnp.broadcast_to(0.25 * patch_grid, (row_count, 2, PATCH_W // 2, 2, feature_width))
    return patch_grid.reshape(4 * pooled_count, feature_width).astype(jnp.bfloat16)

def group_sum(left_side, right_groups):
    left_groups = left_side.astype(jnp.float32).reshape(left_side.shape[0], N_DP, N_SEQ, -1)
    partials = jnp.einsum('rdsc,dsce->sre', left_groups, right_groups)
    rounded = lax.optimization_barrier(partials.astype(jnp.bfloat16)).astype(jnp.float32)
    return lax.optimization_barrier(jnp.sum(rounded, axis=0))

def reference(image_query, image_key, image_value, text_key, text_value, query_gain, key_gain, embed_weight, position_embed, norm_gain, final_gain, up_weight, down_weight, reward_direction):
    input_groups = up_weight.astype(jnp.float32).reshape(N_DP, N_SEQ, -1, EMB)
    output_groups = down_weight.astype(jnp.float32).reshape(N_DP, N_SEQ, -1, EMB)

    def one_sample(sample):
        query_rows, key_rows, value_rows, text_keys, text_values = sample
        queries = norm_heads(query_rows, query_gain)
        key_heads = norm_heads(jnp.concatenate([text_keys, key_rows], axis=0), key_gain)
        value_heads = jnp.concatenate([text_values, value_rows], axis=0).reshape(-1, HEADS, HEAD)
        scores = jnp.einsum('qhd,khd->hqk', queries.astype(jnp.float32), key_heads.astype(jnp.float32)) * HEAD ** (-0.5)
        exponent = jnp.exp(scores)
        attention_weights = (exponent / lax.optimization_barrier(jnp.sum(exponent, axis=-1, keepdims=True))).astype(jnp.bfloat16)
        mixed_heads = jnp.einsum('hqk,khd->qhd', attention_weights.astype(jnp.float32), value_heads.astype(jnp.float32))
        attended = mixed_heads.astype(jnp.bfloat16).reshape(query_rows.shape[0], HD)
        pooled = pool_patches(attended)
        residual_in = jnp.dot(pooled, embed_weight, preferred_element_type=jnp.float32) + position_embed
        normed_in, inverse_in = layer_stats(residual_in)
        hidden_in = (normed_in * norm_gain).astype(jnp.bfloat16)
        preact = jnp.dot(hidden_in, up_weight.T, preferred_element_type=jnp.float32)
        activation, derivative = gelu_parts(preact)
        branch = group_sum(activation.astype(jnp.bfloat16), output_groups)
        residual_out = residual_in + branch
        normed_out, inverse_out = layer_stats(residual_out)
        direction = final_gain * reward_direction
        reward = jnp.mean(lax.optimization_barrier(jnp.sum(normed_out * direction, axis=-1)))
        out_slope = layer_back(direction, normed_out, inverse_out)
        back_slope = jnp.dot(out_slope.astype(jnp.bfloat16), down_weight.T, preferred_element_type=jnp.float32)
        hidden_slope = (back_slope * derivative).astype(jnp.bfloat16)
        slope_in = group_sum(hidden_slope, input_groups)
        input_slope = out_slope + layer_back(slope_in * norm_gain, normed_in, inverse_in)
        pooled_slope = jnp.dot(input_slope.astype(jnp.bfloat16), embed_weight.T, preferred_element_type=jnp.float32)
        return (attended, spread_patches(pooled_slope), reward)
    outputs = lax.map(one_sample, (image_query, image_key, image_value, text_key, text_value))
    return (outputs[0], outputs[1], outputs[2])
```

```python
import functools

import jax
import jax.numpy as jnp
from jax import lax
from jax.experimental import pallas as pl
from jax.experimental.pallas import tpu as pltpu
from jax.sharding import PartitionSpec as P

HEAD = 128
PATCH_W = 32
EPS = 1e-06
ROOT_HALF = 0.7071067811865476
INV_ROOT_TAU = 0.3989422804014327
MESH = pl.DeviceIdType.MESH
F32 = jnp.float32
BF16 = jnp.bfloat16


def norm_head(features, gain):
    wide = features.astype(F32)
    inverse_rms = lax.rsqrt(jnp.mean(wide * wide, axis=-1, keepdims=True) + EPS)
    return (wide * inverse_rms * gain).astype(BF16)


def layer_stats(residual):
    centered = residual - jnp.mean(residual, axis=-1, keepdims=True)
    inverse_std = lax.rsqrt(jnp.mean(centered * centered, axis=-1, keepdims=True) + EPS)
    return centered * inverse_std, inverse_std


def layer_back(upstream, normed, inverse_std):
    return inverse_std * (
        upstream
        - jnp.mean(upstream, axis=-1, keepdims=True)
        - normed * jnp.mean(upstream * normed, axis=-1, keepdims=True)
    )


def gelu_parts(preact):
    cumulative = 0.5 * (1.0 + lax.erf(preact * ROOT_HALF))
    derivative = cumulative + preact * jnp.exp(-0.5 * preact * preact) * INV_ROOT_TAU
    return preact * cumulative, derivative


def dot(left, right):
    return jnp.dot(left, right, preferred_element_type=F32)


def dot_rows(left, right):
    return lax.dot_general(left, right, (((1,), (1,)), ((), ())), preferred_element_type=F32)


def tower_kernel(
    n_dp,
    n_seq,
    gather_here,
    iq_ref,
    ik_ref,
    iv_ref,
    tk_ref,
    tv_ref,
    q_gain_ref,
    k_gain_ref,
    embed_hbm,
    pos_ref,
    norm_gain_ref,
    final_gain_ref,
    up_hbm,
    down_hbm,
    direction_ref,
    attended_ref,
    gradient_ref,
    reward_ref,
    q_buf,
    k_buf,
    v_buf,
    embed,
    up_all,
    down_all,
    pooled_buf,
    resid_in,
    part_buf,
    part_in,
    slope_all,
    part2_buf,
    part2_in,
    slope2_all,
    score_buf,
    local_sem,
    a2a_send,
    a2a_recv,
    w_send,
    w_recv,
    f_send,
    f_recv,
    x_send,
    x_recv,
    s_send,
    s_recv,
):
    dp = lax.axis_index("dp")
    seq = lax.axis_index("seq")
    width = q_buf.shape[2]
    heads = width // HEAD
    img = iq_ref.shape[1]
    txt = tk_ref.shape[1]
    shard = up_hbm.shape[0]
    tokens = resid_in.shape[0]
    mine = tokens // n_seq
    n_chip = n_dp // 2
    core = lax.rem(dp, 2)
    chip = lax.div(dp, 2)

    def peer(d):
        return lax.rem(seq + d, n_seq)

    def source(d):
        return lax.rem(seq + n_seq - d, n_seq)

    def chip_at(d):
        return lax.rem(chip + d, n_chip) * 2 + core

    def chip_from(d):
        return lax.rem(chip + n_chip - d, n_chip) * 2 + core

    sibling = chip * 2 + 1 - core

    def columns(owner):
        return pl.ds(pl.multiple_of(owner * width, HEAD), width)

    def rows(owner, count):
        return pl.ds(pl.multiple_of(owner * count, 16), count)

    def pieces(owner, slot):
        cols = columns(owner)
        return (
            (iq_ref.at[0, :, cols], q_buf.at[slot]),
            (tk_ref.at[0, :, cols], k_buf.at[slot, pl.ds(0, txt)]),
            (ik_ref.at[0, :, cols], k_buf.at[slot, pl.ds(txt, img)]),
            (tv_ref.at[0, :, cols], v_buf.at[slot, pl.ds(0, txt)]),
            (iv_ref.at[0, :, cols], v_buf.at[slot, pl.ds(txt, img)]),
        )

    own_loads = []
    for index, (src, dst) in enumerate(pieces(seq, 0)):
        own_loads.append(pltpu.make_async_copy(src, dst, local_sem.at[index]))
    own_rows = rows(dp, shard) if gather_here else pl.ds(0, shard)
    late_loads = [
        pltpu.make_async_copy(embed_hbm, embed, local_sem.at[5]),
        pltpu.make_async_copy(up_hbm, up_all.at[own_rows], local_sem.at[6]),
        pltpu.make_async_copy(down_hbm, down_all.at[own_rows], local_sem.at[7]),
    ]
    for load in own_loads:
        load.start()

    barrier = pltpu.get_barrier_semaphore()
    partners = 0
    for d in range(1, n_seq):
        pl.semaphore_signal(barrier, inc=1, device_id=(dp, peer(d)), device_id_type=MESH)
        partners += 1
    if gather_here:
        for d in range(1, n_chip):
            pl.semaphore_signal(barrier, inc=1, device_id=(chip_at(d), seq), device_id_type=MESH)
            partners += 1
        pl.semaphore_signal(barrier, inc=1, device_id=(sibling, seq), device_id_type=MESH)
        partners += 1
    pl.semaphore_wait(barrier, partners)

    a2a = {}
    for d in range(1, n_seq):
        for index, (src, dst) in enumerate(pieces(peer(d), d)):
            a2a[d, index] = pltpu.make_async_remote_copy(
                src_ref=src,
                dst_ref=dst,
                send_sem=a2a_send.at[d, index],
                recv_sem=a2a_recv.at[d, index],
                device_id=(dp, peer(d)),
                device_id_type=MESH,
            )
    for index in range(5):
        for d in range(1, n_seq):
            a2a[d, index].start()

    weights, forwards = {}, {}
    if gather_here:
        for index, (src, dst) in enumerate(((up_hbm, up_all), (down_hbm, down_all))):
            for d in range(1, n_chip):
                weights[d, index] = pltpu.make_async_remote_copy(
                    src_ref=src,
                    dst_ref=dst.at[rows(dp, shard)],
                    send_sem=w_send.at[d, index],
                    recv_sem=w_recv.at[d, index],
                    device_id=(chip_at(d), seq),
                    device_id_type=MESH,
                )
                weights[d, index].start()
            for d in range(n_chip):
                held = rows(chip_from(d), shard)
                forwards[d, index] = pltpu.make_async_remote_copy(
                    src_ref=src if d == 0 else dst.at[held],
                    dst_ref=dst.at[held],
                    send_sem=f_send.at[d, index],
                    recv_sem=f_recv.at[d, index],
                    device_id=(sibling, seq),
                    device_id_type=MESH,
                )
            forwards[0, index].start()
    for load in late_loads:
        load.start()
    for load in own_loads:
        load.wait()
    for d in range(1, n_seq):
        a2a[d, 0].wait_recv()

    q_gain = q_gain_ref[...]
    k_gain = k_gain_ref[...]
    queries = []
    for h in range(heads):
        lanes = slice(h * HEAD, (h + 1) * HEAD)
        queries.append(
            jnp.concatenate([norm_head(q_buf[d, :, lanes], q_gain) for d in range(n_seq)], axis=0)
        )
    mixed = [None] * heads
    total = [None] * heads
    for d in range(n_seq):
        if d:
            for index in range(1, 5):
                a2a[d, index].wait_recv()
        for h in range(heads):
            lanes = slice(h * HEAD, (h + 1) * HEAD)
            keys = norm_head(k_buf[d, :, lanes], k_gain)
            exponent = jnp.exp(dot_rows(queries[h], keys) * HEAD**-0.5)
            part_total = jnp.sum(exponent, axis=-1, keepdims=True)
            part_mixed = dot(exponent.astype(BF16), v_buf[d, :, lanes])
            total[h] = part_total if d == 0 else total[h] + part_total
            mixed[h] = part_mixed if d == 0 else mixed[h] + part_mixed
    for h in range(heads):
        lanes = slice(h * HEAD, (h + 1) * HEAD)
        done = (mixed[h] / total[h]).astype(BF16)
        for d in range(n_seq):
            attended_ref[rows(source(d), img), lanes] = done[d * img : (d + 1) * img]

    def pool_map(shape, token_axis):
        token = lax.broadcasted_iota(jnp.int32, shape, token_axis)
        pool = lax.broadcasted_iota(jnp.int32, shape, 1 - token_axis)
        place = lax.div(token, 2 * PATCH_W) * (PATCH_W // 2) + lax.div(lax.rem(token, PATCH_W), 2)
        return jnp.where(place == pool, 0.25, 0.0).astype(BF16)

    image_tokens = attended_ref.shape[0]
    pooled = dot(pool_map((tokens, image_tokens), 1), attended_ref[...])
    pooled_buf[0] = pooled.astype(BF16)

    def spread_to(kind, src_of, dst_of):
        copies = {}
        for d in range(1, n_seq):
            copies[d] = pltpu.make_async_remote_copy(
                src_ref=src_of(d),
                dst_ref=dst_of(d),
                send_sem=x_send.at[kind, d],
                recv_sem=x_recv.at[kind, d],
                device_id=(dp, peer(d)),
                device_id_type=MESH,
            )
            copies[d].start()
        return copies

    pooled_copies = spread_to(0, lambda d: pooled_buf.at[0], lambda d: pooled_buf.at[d])
    for load in late_loads:
        load.wait()
    if gather_here:
        for index in range(2):
            for d in range(1, n_chip):
                weights[d, index].wait_recv()
                forwards[d, index].start()

    residual = pos_ref[...]
    for d in range(n_seq):
        if d:
            pooled_copies[d].wait_recv()
        residual = residual + dot(pooled_buf[d], embed[rows(source(d), width), :])
    resid_in[...] = residual
    normed_in, _ = layer_stats(residual)
    norm_gain = norm_gain_ref[...]
    hidden_in = (normed_in * norm_gain).astype(BF16)
    if gather_here:
        for d in range(n_chip):
            forwards[d, 0].wait_recv()
    activation, derivative = gelu_parts(dot_rows(hidden_in, up_all[...]))
    if gather_here:
        for d in range(n_chip):
            forwards[d, 1].wait_recv()
    part_buf[...] = dot(activation.astype(BF16), down_all[...]).astype(BF16)
    part_copies = spread_to(
        1, lambda d: part_buf.at[rows(peer(d), mine)], lambda d: part_in.at[d]
    )
    own_resid = resid_in[rows(seq, mine), :]
    normed_own, inverse_own = layer_stats(own_resid)
    branch = part_buf[rows(seq, mine), :].astype(F32)
    for d in range(1, n_seq):
        part_copies[d].wait_recv()
        branch = branch + part_in[d].astype(F32)
    normed_out, inverse_out = layer_stats(own_resid + branch)
    direction = final_gain_ref[...] * direction_ref[...]
    out_slope = layer_back(direction, normed_out, inverse_out)
    slope_all[rows(seq, mine), :] = out_slope.astype(BF16)
    own_tokens = rows(seq, mine)
    slope_copies = spread_to(
        2, lambda d: slope_all.at[own_tokens], lambda d: slope_all.at[own_tokens]
    )
    score = jnp.sum(jnp.sum(normed_out * direction, axis=-1, keepdims=True), axis=0, keepdims=True)
    score_buf[0] = jnp.broadcast_to(score, score_buf.shape[1:])
    score_copies = {}
    for d in range(1, n_seq):
        score_copies[d] = pltpu.make_async_remote_copy(
            src_ref=score_buf.at[0],
            dst_ref=score_buf.at[d],
            send_sem=s_send.at[d],
            recv_sem=s_recv.at[d],
            device_id=(dp, peer(d)),
            device_id_type=MESH,
        )
        score_copies[d].start()

    for d in range(1, n_seq):
        slope_copies[d].wait_recv()
    back = dot_rows(slope_all[...], down_all[...])
    part2_buf[...] = dot((back * derivative).astype(BF16), up_all[...]).astype(BF16)
    part2_copies = spread_to(
        3, lambda d: part2_buf.at[rows(peer(d), mine)], lambda d: part2_in.at[d]
    )
    slope_in = part2_buf[rows(seq, mine), :].astype(F32)
    for d in range(1, n_seq):
        part2_copies[d].wait_recv()
        slope_in = slope_in + part2_in[d].astype(F32)
    input_slope = out_slope + layer_back(slope_in * norm_gain, normed_own, inverse_own)
    slope2_all[rows(seq, mine), :] = input_slope.astype(BF16)
    slope2_copies = spread_to(
        4, lambda d: slope2_all.at[own_tokens], lambda d: slope2_all.at[own_tokens]
    )
    score_sum = score_buf[0]
    for d in range(1, n_seq):
        score_copies[d].wait_recv()
        score_sum = score_sum + score_buf[d]
    reward_ref[...] = score_sum * (1.0 / tokens)
    for d in range(1, n_seq):
        slope2_copies[d].wait_recv()
    pooled_slope = dot_rows(slope2_all[...], embed[rows(seq, width), :]).astype(BF16)
    gradient_ref[...] = dot(pool_map((image_tokens, tokens), 0), pooled_slope).astype(BF16)

    for group in (
        a2a,
        weights,
        forwards,
        pooled_copies,
        part_copies,
        slope_copies,
        score_copies,
        part2_copies,
        slope2_copies,
    ):
        for copy in group.values():
            copy.wait_send()


def on_device(
    n_dp,
    n_seq,
    image_query,
    image_key,
    image_value,
    text_key,
    text_value,
    query_gain,
    key_gain,
    embed_weight,
    position_embed,
    norm_gain,
    final_gain,
    up_weight,
    down_weight,
    reward_direction,
):
    gather_here = n_dp % 2 == 0 and n_dp <= 16 and up_weight.shape[0] % 16 == 0
    if not gather_here:
        up_weight = lax.all_gather(up_weight, "dp", axis=0, tiled=True)
        down_weight = lax.all_gather(down_weight, "dp", axis=0, tiled=True)
    img, txt = image_query.shape[1], text_key.shape[1]
    features, emb = embed_weight.shape
    width = features // n_seq
    tokens = position_embed.shape[0]
    mine = tokens // n_seq
    hidden = up_weight.shape[0] * (n_dp if gather_here else 1)
    n_chip = n_dp // 2 if gather_here else 1
    keys = img + txt
    vmem = pl.BlockSpec(memory_space=pltpu.VMEM)
    anywhere = pl.BlockSpec(memory_space=pl.ANY)
    dma = pltpu.SemaphoreType.DMA
    attended, gradient, reward = pl.pallas_call(
        functools.partial(tower_kernel, n_dp, n_seq, gather_here),
        out_shape=(
            jax.ShapeDtypeStruct((img * n_seq, width), BF16),
            jax.ShapeDtypeStruct((img * n_seq, width), BF16),
            jax.ShapeDtypeStruct((8, 128), F32),
        ),
        in_specs=[anywhere] * 5
        + [vmem] * 2
        + [anywhere]
        + [vmem] * 3
        + [anywhere] * 2
        + [vmem],
        out_specs=(vmem, vmem, vmem),
        scratch_shapes=[
            pltpu.VMEM((n_seq, img, width), BF16),
            pltpu.VMEM((n_seq, keys, width), BF16),
            pltpu.VMEM((n_seq, keys, width), BF16),
            pltpu.VMEM((features, emb), BF16),
            pltpu.VMEM((hidden, emb), BF16),
            pltpu.VMEM((hidden, emb), BF16),
            pltpu.VMEM((n_seq, tokens, width), BF16),
            pltpu.VMEM((tokens, emb), F32),
            pltpu.VMEM((tokens, emb), BF16),
            pltpu.VMEM((n_seq, mine, emb), BF16),
            pltpu.VMEM((tokens, emb), BF16),
            pltpu.VMEM((tokens, emb), BF16),
            pltpu.VMEM((n_seq, mine, emb), BF16),
            pltpu.VMEM((tokens, emb), BF16),
            pltpu.VMEM((n_seq, 8, 128), F32),
            dma((8,)),
            dma((n_seq, 5)),
            dma((n_seq, 5)),
            dma((n_chip, 2)),
            dma((n_chip, 2)),
            dma((n_chip, 2)),
            dma((n_chip, 2)),
            dma((5, n_seq)),
            dma((5, n_seq)),
            dma((n_seq,)),
            dma((n_seq,)),
        ],
        compiler_params=pltpu.CompilerParams(
            collective_id=0, has_side_effects=True, vmem_limit_bytes=40 * 1024 * 1024
        ),
    )(
        image_query,
        image_key,
        image_value,
        text_key,
        text_value,
        query_gain.reshape(1, -1),
        key_gain.reshape(1, -1),
        embed_weight,
        position_embed,
        norm_gain.reshape(1, -1),
        final_gain.reshape(1, -1),
        up_weight,
        down_weight,
        reward_direction.reshape(1, -1),
    )
    return attended[None], gradient[None], reward[0, :1]


def solution(mesh):
    return jax.shard_map(
        functools.partial(on_device, mesh.shape["dp"], mesh.shape["seq"]),
        mesh=mesh,
        in_specs=(
            P("dp", "seq", None),
            P("dp", "seq", None),
            P("dp", "seq", None),
            P("dp", "seq", None),
            P("dp", "seq", None),
            P(),
            P(),
            P(),
            P(),
            P(),
            P(),
            P(("dp", "seq"), None),
            P(("dp", "seq"), None),
            P(),
        ),
        out_specs=(P("dp", None, "seq"), P("dp", None, "seq"), P("dp")),
        check_vma=False,
    )
```

```python
import functools

import jax
import jax.numpy as jnp
from jax import lax
from jax.experimental import pallas as pl
from jax.experimental.pallas import tpu as pltpu
from jax.sharding import PartitionSpec as P

HEAD = 128
PATCH_W = 32
EPS = 1e-06
ROOT_HALF = 0.7071067811865476
INV_ROOT_TAU = 0.3989422804014327
MESH = pl.DeviceIdType.MESH
F32 = jnp.float32
BF16 = jnp.bfloat16


def norm_head(features, gain):
    wide = features.astype(F32)
    inverse_rms = lax.rsqrt(jnp.mean(wide * wide, axis=-1, keepdims=True) + EPS)
    return (wide * inverse_rms * gain).astype(BF16)


def layer_stats(residual):
    centered = residual - jnp.mean(residual, axis=-1, keepdims=True)
    inverse_std = lax.rsqrt(jnp.mean(centered * centered, axis=-1, keepdims=True) + EPS)
    return centered * inverse_std, inverse_std


def layer_back(upstream, normed, inverse_std):
    return inverse_std * (
        upstream
        - jnp.mean(upstream, axis=-1, keepdims=True)
        - normed * jnp.mean(upstream * normed, axis=-1, keepdims=True)
    )


def gelu_parts(preact):
    cumulative = 0.5 * (1.0 + lax.erf(preact * ROOT_HALF))
    derivative = cumulative + preact * jnp.exp(-0.5 * preact * preact) * INV_ROOT_TAU
    return preact * cumulative, derivative


def dot(left, right):
    return jnp.dot(left, right, preferred_element_type=F32)


def dot_rows(left, right):
    return lax.dot_general(left, right, (((1,), (1,)), ((), ())), preferred_element_type=F32)


def pool_map(shape, token_axis):
    token = lax.broadcasted_iota(jnp.int32, shape, token_axis)
    pool = lax.broadcasted_iota(jnp.int32, shape, 1 - token_axis)
    place = lax.div(token, 2 * PATCH_W) * (PATCH_W // 2) + lax.div(lax.rem(token, PATCH_W), 2)
    return jnp.where(place == pool, 0.25, 0.0).astype(BF16)


def finish_kernel(attended_ref, slope_ref, attended_out, gradient_ref):
    attended_out[...] = attended_ref[...]
    shape = (gradient_ref.shape[0], slope_ref.shape[0])
    gradient_ref[...] = dot(pool_map(shape, 0), slope_ref[...]).astype(BF16)


def tower_kernel(
    n_dp,
    n_seq,
    gather_here,
    iq_ref,
    ik_ref,
    iv_ref,
    tk_ref,
    tv_ref,
    q_gain_hbm,
    k_gain_hbm,
    embed_hbm,
    pos_hbm,
    norm_gain_hbm,
    final_gain_hbm,
    up_hbm,
    down_hbm,
    direction_hbm,
    attended_ref,
    slope_ref,
    reward_ref,
    q_buf,
    k_buf,
    v_buf,
    q_gain_ref,
    k_gain_ref,
    pos_ref,
    norm_gain_ref,
    final_gain_ref,
    direction_ref,
    embed,
    up_all,
    down_all,
    pooled_buf,
    resid_in,
    part_buf,
    part_in,
    slope_all,
    part2_buf,
    part2_in,
    slope2_out,
    slope2_in,
    score_buf,
    local_sem,
    a2a_send,
    a2a_recv,
    w_send,
    w_recv,
    f_send,
    f_recv,
    x_send,
    x_recv,
    s_send,
    s_recv,
):
    dp = lax.axis_index("dp")
    seq = lax.axis_index("seq")
    width = q_buf.shape[2]
    heads = width // HEAD
    img = iq_ref.shape[1]
    txt = tk_ref.shape[1]
    shard = up_hbm.shape[0]
    tokens = resid_in.shape[0]
    mine = tokens // n_seq
    n_chip = n_dp // 2
    core = lax.rem(dp, 2)
    chip = lax.div(dp, 2)

    def peer(d):
        return lax.rem(seq + d, n_seq)

    def source(d):
        return lax.rem(seq + n_seq - d, n_seq)

    def chip_at(d):
        return lax.rem(chip + d, n_chip) * 2 + core

    def chip_from(d):
        return lax.rem(chip + n_chip - d, n_chip) * 2 + core

    sibling = chip * 2 + 1 - core

    def columns(owner):
        return pl.ds(pl.multiple_of(owner * width, HEAD), width)

    def rows(owner, count):
        return pl.ds(pl.multiple_of(owner * count, 16), count)

    def pieces(owner, slot):
        cols = columns(owner)
        return (
            (iq_ref.at[0, :, cols], q_buf.at[slot]),
            (tk_ref.at[0, :, cols], k_buf.at[slot, pl.ds(0, txt)]),
            (ik_ref.at[0, :, cols], k_buf.at[slot, pl.ds(txt, img)]),
            (tv_ref.at[0, :, cols], v_buf.at[slot, pl.ds(0, txt)]),
            (iv_ref.at[0, :, cols], v_buf.at[slot, pl.ds(txt, img)]),
        )

    own_loads = []
    for index, (src, dst) in enumerate(pieces(seq, 0)):
        own_loads.append(pltpu.make_async_copy(src, dst, local_sem.at[index]))
    for index, (src, dst) in enumerate(((q_gain_hbm, q_gain_ref), (k_gain_hbm, k_gain_ref))):
        own_loads.append(pltpu.make_async_copy(src, dst, local_sem.at[8 + index]))
    own_rows = rows(dp, shard) if gather_here else pl.ds(0, shard)
    late_loads = [
        pltpu.make_async_copy(embed_hbm, embed, local_sem.at[5]),
        pltpu.make_async_copy(up_hbm, up_all.at[own_rows], local_sem.at[6]),
        pltpu.make_async_copy(down_hbm, down_all.at[own_rows], local_sem.at[7]),
        pltpu.make_async_copy(pos_hbm, pos_ref, local_sem.at[10]),
        pltpu.make_async_copy(norm_gain_hbm, norm_gain_ref, local_sem.at[11]),
        pltpu.make_async_copy(final_gain_hbm, final_gain_ref, local_sem.at[12]),
        pltpu.make_async_copy(direction_hbm, direction_ref, local_sem.at[13]),
    ]
    for load in own_loads:
        load.start()

    barrier = pltpu.get_barrier_semaphore()
    partners = 0
    for d in range(1, n_seq):
        pl.semaphore_signal(barrier, inc=1, device_id=(dp, peer(d)), device_id_type=MESH)
        partners += 1
    if gather_here:
        for d in range(1, n_chip):
            pl.semaphore_signal(barrier, inc=1, device_id=(chip_at(d), seq), device_id_type=MESH)
            partners += 1
        pl.semaphore_signal(barrier, inc=1, device_id=(sibling, seq), device_id_type=MESH)
        partners += 1
    pl.semaphore_wait(barrier, partners)

    a2a = {}
    for d in range(1, n_seq):
        for index, (src, dst) in enumerate(pieces(peer(d), d)):
            a2a[d, index] = pltpu.make_async_remote_copy(
                src_ref=src,
                dst_ref=dst,
                send_sem=a2a_send.at[d, index],
                recv_sem=a2a_recv.at[d, index],
                device_id=(dp, peer(d)),
                device_id_type=MESH,
            )
    for index in range(5):
        for d in range(1, n_seq):
            a2a[d, index].start()

    weights, forwards = {}, {}
    if gather_here:
        for index, (src, dst) in enumerate(((up_hbm, up_all), (down_hbm, down_all))):
            for d in range(1, n_chip):
                weights[d, index] = pltpu.make_async_remote_copy(
                    src_ref=src,
                    dst_ref=dst.at[rows(dp, shard)],
                    send_sem=w_send.at[d, index],
                    recv_sem=w_recv.at[d, index],
                    device_id=(chip_at(d), seq),
                    device_id_type=MESH,
                )
                weights[d, index].start()
            for d in range(n_chip):
                held = rows(chip_from(d), shard)
                forwards[d, index] = pltpu.make_async_remote_copy(
                    src_ref=src if d == 0 else dst.at[held],
                    dst_ref=dst.at[held],
                    send_sem=f_send.at[d, index],
                    recv_sem=f_recv.at[d, index],
                    device_id=(sibling, seq),
                    device_id_type=MESH,
                )
            forwards[0, index].start()
    for load in late_loads:
        load.start()
    for load in own_loads:
        load.wait()
    for d in range(1, n_seq):
        a2a[d, 0].wait_recv()

    q_gain = q_gain_ref[...].reshape(1, -1)
    k_gain = k_gain_ref[...].reshape(1, -1)
    queries = []
    for h in range(heads):
        lanes = slice(h * HEAD, (h + 1) * HEAD)
        queries.append(
            jnp.concatenate([norm_head(q_buf[d, :, lanes], q_gain) for d in range(n_seq)], axis=0)
        )
    mixed = [None] * heads
    total = [None] * heads
    for d in range(n_seq):
        if d:
            for index in range(1, 5):
                a2a[d, index].wait_recv()
        for h in range(heads):
            lanes = slice(h * HEAD, (h + 1) * HEAD)
            keys = norm_head(k_buf[d, :, lanes], k_gain)
            exponent = jnp.exp(dot_rows(queries[h], keys) * HEAD**-0.5)
            part_total = jnp.sum(exponent, axis=-1, keepdims=True)
            part_mixed = dot(exponent.astype(BF16), v_buf[d, :, lanes])
            total[h] = part_total if d == 0 else total[h] + part_total
            mixed[h] = part_mixed if d == 0 else mixed[h] + part_mixed
    for h in range(heads):
        lanes = slice(h * HEAD, (h + 1) * HEAD)
        done = (mixed[h] / total[h]).astype(BF16)
        for d in range(n_seq):
            attended_ref[rows(source(d), img), lanes] = done[d * img : (d + 1) * img]

    image_tokens = attended_ref.shape[0]
    pooled = dot(pool_map((tokens, image_tokens), 1), attended_ref[...])
    pooled_buf[0] = pooled.astype(BF16)

    def spread_to(kind, src_of, dst_of):
        copies = {}
        for d in range(1, n_seq):
            copies[d] = pltpu.make_async_remote_copy(
                src_ref=src_of(d),
                dst_ref=dst_of(d),
                send_sem=x_send.at[kind, d],
                recv_sem=x_recv.at[kind, d],
                device_id=(dp, peer(d)),
                device_id_type=MESH,
            )
            copies[d].start()
        return copies

    pooled_copies = spread_to(0, lambda d: pooled_buf.at[0], lambda d: pooled_buf.at[d])
    for load in late_loads:
        load.wait()
    if gather_here:
        for index in range(2):
            for d in range(1, n_chip):
                weights[d, index].wait_recv()
                forwards[d, index].start()

    residual = pos_ref[...]
    for d in range(n_seq):
        if d:
            pooled_copies[d].wait_recv()
        residual = residual + dot(pooled_buf[d], embed[rows(source(d), width), :])
    resid_in[...] = residual
    normed_in, _ = layer_stats(residual)
    norm_gain = norm_gain_ref[...].reshape(1, -1)
    hidden_in = (normed_in * norm_gain).astype(BF16)
    if gather_here:
        for d in range(n_chip):
            forwards[d, 0].wait_recv()
    activation, derivative = gelu_parts(dot_rows(hidden_in, up_all[...]))
    if gather_here:
        for d in range(n_chip):
            forwards[d, 1].wait_recv()
    part_buf[...] = dot(activation.astype(BF16), down_all[...]).astype(BF16)
    part_copies = spread_to(
        1, lambda d: part_buf.at[rows(peer(d), mine)], lambda d: part_in.at[d]
    )
    own_resid = resid_in[rows(seq, mine), :]
    normed_own, inverse_own = layer_stats(own_resid)
    branch = part_buf[rows(seq, mine), :].astype(F32)
    for d in range(1, n_seq):
        part_copies[d].wait_recv()
        branch = branch + part_in[d].astype(F32)
    normed_out, inverse_out = layer_stats(own_resid + branch)
    direction = (final_gain_ref[...] * direction_ref[...]).reshape(1, -1)
    out_slope = layer_back(direction, normed_out, inverse_out)
    slope_all[rows(seq, mine), :] = out_slope.astype(BF16)
    own_tokens = rows(seq, mine)
    slope_copies = spread_to(
        2, lambda d: slope_all.at[own_tokens], lambda d: slope_all.at[own_tokens]
    )
    score = jnp.sum(jnp.sum(normed_out * direction, axis=-1, keepdims=True), axis=0, keepdims=True)
    score_buf[0] = jnp.broadcast_to(score, score_buf.shape[1:])
    score_copies = {}
    for d in range(1, n_seq):
        score_copies[d] = pltpu.make_async_remote_copy(
            src_ref=score_buf.at[0],
            dst_ref=score_buf.at[d],
            send_sem=s_send.at[d],
            recv_sem=s_recv.at[d],
            device_id=(dp, peer(d)),
            device_id_type=MESH,
        )
        score_copies[d].start()

    for d in range(1, n_seq):
        slope_copies[d].wait_recv()
    back = dot_rows(slope_all[...], down_all[...])
    part2_buf[...] = dot((back * derivative).astype(BF16), up_all[...]).astype(BF16)
    part2_copies = spread_to(
        3, lambda d: part2_buf.at[rows(peer(d), mine)], lambda d: part2_in.at[d]
    )
    slope_in = part2_buf[rows(seq, mine), :].astype(F32)
    for d in range(1, n_seq):
        part2_copies[d].wait_recv()
        slope_in = slope_in + part2_in[d].astype(F32)
    input_slope = out_slope + layer_back(slope_in * norm_gain, normed_own, inverse_own)
    pooled_own = dot_rows(input_slope.astype(BF16), embed[...]).astype(BF16)
    for owner in range(n_seq):
        slope2_out[owner] = pooled_own[:, owner * width : (owner + 1) * width]
    slope2_in[rows(seq, mine), :] = slope2_out[seq]
    slope2_copies = spread_to(
        4, lambda d: slope2_out.at[peer(d)], lambda d: slope2_in.at[own_tokens]
    )
    score_sum = score_buf[0]
    for d in range(1, n_seq):
        score_copies[d].wait_recv()
        score_sum = score_sum + score_buf[d]
    reward_ref[0] = score_sum[0, 0] * (1.0 / tokens)
    for d in range(1, n_seq):
        slope2_copies[d].wait_recv()
    slope_ref[...] = slope2_in[...]

    for group in (
        a2a,
        weights,
        forwards,
        pooled_copies,
        part_copies,
        slope_copies,
        score_copies,
        part2_copies,
        slope2_copies,
    ):
        for copy in group.values():
            copy.wait_send()


def on_device(
    n_dp,
    n_seq,
    image_query,
    image_key,
    image_value,
    text_key,
    text_value,
    query_gain,
    key_gain,
    embed_weight,
    position_embed,
    norm_gain,
    final_gain,
    up_weight,
    down_weight,
    reward_direction,
):
    gather_here = n_dp % 2 == 0 and n_dp <= 16 and up_weight.shape[0] % 16 == 0
    if not gather_here:
        up_weight = lax.all_gather(up_weight, "dp", axis=0, tiled=True)
        down_weight = lax.all_gather(down_weight, "dp", axis=0, tiled=True)
    img, txt = image_query.shape[1], text_key.shape[1]
    features, emb = embed_weight.shape
    width = features // n_seq
    tokens = position_embed.shape[0]
    mine = tokens // n_seq
    hidden = up_weight.shape[0] * (n_dp if gather_here else 1)
    n_chip = n_dp // 2 if gather_here else 1
    keys = img + txt
    vmem = pl.BlockSpec(memory_space=pltpu.VMEM)
    dma = pltpu.SemaphoreType.DMA
    attended, slope, reward = pl.pallas_call(
        functools.partial(tower_kernel, n_dp, n_seq, gather_here),
        out_shape=(
            jax.ShapeDtypeStruct((img * n_seq, width), BF16),
            jax.ShapeDtypeStruct((tokens, width), BF16),
            jax.ShapeDtypeStruct((1,), F32),
        ),
        in_specs=[pl.BlockSpec(memory_space=pltpu.HBM)] * 14,
        out_specs=(vmem, vmem, pl.BlockSpec(memory_space=pltpu.SMEM)),
        scratch_shapes=[
            pltpu.VMEM((n_seq, img, width), BF16),
            pltpu.VMEM((n_seq, keys, width), BF16),
            pltpu.VMEM((n_seq, keys, width), BF16),
            pltpu.VMEM((HEAD,), F32),
            pltpu.VMEM((HEAD,), F32),
            pltpu.VMEM((tokens, emb), F32),
            pltpu.VMEM((emb,), F32),
            pltpu.VMEM((emb,), F32),
            pltpu.VMEM((emb,), F32),
            pltpu.VMEM((features, emb), BF16),
            pltpu.VMEM((hidden, emb), BF16),
            pltpu.VMEM((hidden, emb), BF16),
            pltpu.VMEM((n_seq, tokens, width), BF16),
            pltpu.VMEM((tokens, emb), F32),
            pltpu.VMEM((tokens, emb), BF16),
            pltpu.VMEM((n_seq, mine, emb), BF16),
            pltpu.VMEM((tokens, emb), BF16),
            pltpu.VMEM((tokens, emb), BF16),
            pltpu.VMEM((n_seq, mine, emb), BF16),
            pltpu.VMEM((n_seq, mine, width), BF16),
            pltpu.VMEM((tokens, width), BF16),
            pltpu.VMEM((n_seq, 8, 128), F32),
            dma((14,)),
            dma((n_seq, 5)),
            dma((n_seq, 5)),
            dma((n_chip, 2)),
            dma((n_chip, 2)),
            dma((n_chip, 2)),
            dma((n_chip, 2)),
            dma((5, n_seq)),
            dma((5, n_seq)),
            dma((n_seq,)),
            dma((n_seq,)),
        ],
        compiler_params=pltpu.CompilerParams(
            collective_id=0, has_side_effects=True, vmem_limit_bytes=(64 * 1024 - 256) * 1024
        ),
    )(
        image_query,
        image_key,
        image_value,
        text_key,
        text_value,
        query_gain,
        key_gain,
        embed_weight,
        position_embed,
        norm_gain,
        final_gain,
        up_weight,
        down_weight,
        reward_direction,
    )
    result = jax.ShapeDtypeStruct((img * n_seq, width), BF16)
    attended, gradient = pl.pallas_call(
        finish_kernel,
        out_shape=(result, result),
        in_specs=[vmem, vmem],
        out_specs=(vmem, vmem),
    )(attended, slope)
    return attended[None], gradient[None], reward


def solution(mesh):
    return jax.shard_map(
        functools.partial(on_device, mesh.shape["dp"], mesh.shape["seq"]),
        mesh=mesh,
        in_specs=(
            P("dp", "seq", None),
            P("dp", "seq", None),
            P("dp", "seq", None),
            P("dp", "seq", None),
            P("dp", "seq", None),
            P(),
            P(),
            P(),
            P(),
            P(),
            P(),
            P(("dp", "seq"), None),
            P(("dp", "seq"), None),
            P(),
        ),
        out_specs=(P("dp", None, "seq"), P("dp", None, "seq"), P("dp")),
        check_vma=False,
    )
```

```python
import functools

import jax
import jax.numpy as jnp
from jax import lax
from jax.experimental import pallas as pl
from jax.experimental.pallas import tpu as pltpu
from jax.sharding import PartitionSpec as P

HEAD = 128
PATCH_W = 32
EPS = 1e-06
ROOT_HALF = 0.7071067811865476
INV_ROOT_TAU = 0.3989422804014327
MESH = pl.DeviceIdType.MESH
F32 = jnp.float32
BF16 = jnp.bfloat16


def norm_head(features, gain):
    wide = features.astype(F32)
    inverse_rms = lax.rsqrt(jnp.mean(wide * wide, axis=-1, keepdims=True) + EPS)
    return (wide * inverse_rms * gain).astype(BF16)


def layer_stats(residual):
    centered = residual - jnp.mean(residual, axis=-1, keepdims=True)
    inverse_std = lax.rsqrt(jnp.mean(centered * centered, axis=-1, keepdims=True) + EPS)
    return centered * inverse_std, inverse_std


def layer_back(upstream, normed, inverse_std):
    return inverse_std * (
        upstream
        - jnp.mean(upstream, axis=-1, keepdims=True)
        - normed * jnp.mean(upstream * normed, axis=-1, keepdims=True)
    )


def gelu_parts(preact):
    cumulative = 0.5 * (1.0 + lax.erf(preact * ROOT_HALF))
    derivative = cumulative + preact * jnp.exp(-0.5 * preact * preact) * INV_ROOT_TAU
    return preact * cumulative, derivative


def dot(left, right):
    return jnp.dot(left, right, preferred_element_type=F32)


def dot_rows(left, right):
    return lax.dot_general(left, right, (((1,), (1,)), ((), ())), preferred_element_type=F32)


def pool_map(shape, token_axis):
    token = lax.broadcasted_iota(jnp.int32, shape, token_axis)
    pool = lax.broadcasted_iota(jnp.int32, shape, 1 - token_axis)
    place = lax.div(token, 2 * PATCH_W) * (PATCH_W // 2) + lax.div(lax.rem(token, PATCH_W), 2)
    return jnp.where(place == pool, 0.25, 0.0).astype(BF16)


def finish_kernel(attended_ref, slope_ref, attended_out, gradient_ref):
    attended_out[...] = attended_ref[...]
    shape = (gradient_ref.shape[0], slope_ref.shape[0])
    gradient_ref[...] = dot(pool_map(shape, 0), slope_ref[...]).astype(BF16)


def tower_kernel(
    n_dp,
    n_seq,
    gather_here,
    iq_ref,
    ik_ref,
    iv_ref,
    tk_ref,
    tv_ref,
    q_gain_hbm,
    k_gain_hbm,
    embed_hbm,
    pos_hbm,
    norm_gain_hbm,
    final_gain_hbm,
    up_hbm,
    down_hbm,
    direction_hbm,
    attended_ref,
    slope_ref,
    reward_ref,
    q_buf,
    k_buf,
    v_buf,
    mix_out,
    mix_in,
    total_out,
    total_in,
    q_gain_ref,
    k_gain_ref,
    pos_ref,
    norm_gain_ref,
    final_gain_ref,
    direction_ref,
    embed,
    up_all,
    down_all,
    pooled_buf,
    resid_in,
    part_buf,
    part_in,
    slope_all,
    part2_buf,
    part2_in,
    slope2_out,
    slope2_in,
    score_buf,
    local_sem,
    q_send,
    q_recv,
    kv_send,
    kv_recv,
    mix_send,
    mix_recv,
    w_send,
    w_recv,
    f_send,
    f_recv,
    x_send,
    x_recv,
    s_send,
    s_recv,
):
    dp = lax.axis_index("dp")
    seq = lax.axis_index("seq")
    width = q_buf.shape[3]
    heads = width // HEAD
    img = iq_ref.shape[1]
    txt = tk_ref.shape[1]
    shard = up_hbm.shape[0]
    tokens = resid_in.shape[0]
    mine = tokens // n_seq
    n_chip = n_dp // 2
    half = n_seq // 2
    place = lax.rem(seq, half)
    base = seq - place
    core = lax.rem(dp, 2)
    chip = lax.div(dp, 2)

    def peer(d):
        return lax.rem(seq + d, n_seq)

    def source(d):
        return lax.rem(seq + n_seq - d, n_seq)

    def chip_at(d):
        return lax.rem(chip + d, n_chip) * 2 + core

    def chip_from(d):
        return lax.rem(chip + n_chip - d, n_chip) * 2 + core

    sibling = chip * 2 + 1 - core

    def columns(owner):
        return pl.ds(pl.multiple_of(owner * width, HEAD), width)

    def rows(owner, count):
        return pl.ds(pl.multiple_of(owner * count, 16), count)

    def group(owner, which):
        return columns(owner if which else lax.rem(owner + half, n_seq))

    def query_piece(owner, which):
        return iq_ref.at[0, :, group(owner, which)], q_buf.at[seq, which]

    def key_pieces(owner, which, slot):
        cols = group(owner, which)
        return (
            (tk_ref.at[0, :, cols], k_buf.at[slot, which, pl.ds(0, txt)]),
            (ik_ref.at[0, :, cols], k_buf.at[slot, which, pl.ds(txt, img)]),
            (tv_ref.at[0, :, cols], v_buf.at[slot, which, pl.ds(0, txt)]),
            (iv_ref.at[0, :, cols], v_buf.at[slot, which, pl.ds(txt, img)]),
        )

    own_loads = []
    for which in range(2):
        for src, dst in (query_piece(seq, which), *key_pieces(seq, which, 0)):
            index = 14 + len(own_loads)
            own_loads.append(pltpu.make_async_copy(src, dst, local_sem.at[index]))
    for index, (src, dst) in enumerate(((q_gain_hbm, q_gain_ref), (k_gain_hbm, k_gain_ref))):
        own_loads.append(pltpu.make_async_copy(src, dst, local_sem.at[8 + index]))
    own_rows = rows(dp, shard) if gather_here else pl.ds(0, shard)
    late_loads = [
        pltpu.make_async_copy(embed_hbm, embed, local_sem.at[5]),
        pltpu.make_async_copy(up_hbm, up_all.at[own_rows], local_sem.at[6]),
        pltpu.make_async_copy(down_hbm, down_all.at[own_rows], local_sem.at[7]),
        pltpu.make_async_copy(pos_hbm, pos_ref, local_sem.at[10]),
        pltpu.make_async_copy(norm_gain_hbm, norm_gain_ref, local_sem.at[11]),
        pltpu.make_async_copy(final_gain_hbm, final_gain_ref, local_sem.at[12]),
        pltpu.make_async_copy(direction_hbm, direction_ref, local_sem.at[13]),
    ]
    for load in own_loads:
        load.start()

    barrier = pltpu.get_barrier_semaphore()
    partners = 0
    for d in range(1, n_seq):
        pl.semaphore_signal(barrier, inc=1, device_id=(dp, peer(d)), device_id_type=MESH)
        partners += 1
    if gather_here:
        for d in range(1, n_chip):
            pl.semaphore_signal(barrier, inc=1, device_id=(chip_at(d), seq), device_id_type=MESH)
            partners += 1
        pl.semaphore_signal(barrier, inc=1, device_id=(sibling, seq), device_id_type=MESH)
        partners += 1
    pl.semaphore_wait(barrier, partners)

    a2a = {}
    for which in range(2):
        for d in range(1, n_seq):
            src, dst = query_piece(peer(d), which)
            a2a[d, which] = pltpu.make_async_remote_copy(
                src_ref=src,
                dst_ref=dst,
                send_sem=q_send.at[d, which],
                recv_sem=q_recv.at[d, which],
                device_id=(dp, peer(d)),
                device_id_type=MESH,
            )
            a2a[d, which].start()
        for e in range(1, half):
            target = base + lax.rem(place + e, half)
            for index, (src, dst) in enumerate(key_pieces(target, which, e)):
                a2a[e, which, index] = pltpu.make_async_remote_copy(
                    src_ref=src,
                    dst_ref=dst,
                    send_sem=kv_send.at[e, which, index],
                    recv_sem=kv_recv.at[e, which, index],
                    device_id=(dp, target),
                    device_id_type=MESH,
                )
                a2a[e, which, index].start()

    weights, forwards = {}, {}
    if gather_here:
        for index, (src, dst) in enumerate(((up_hbm, up_all), (down_hbm, down_all))):
            for d in range(1, n_chip):
                weights[d, index] = pltpu.make_async_remote_copy(
                    src_ref=src,
                    dst_ref=dst.at[rows(dp, shard)],
                    send_sem=w_send.at[d, index],
                    recv_sem=w_recv.at[d, index],
                    device_id=(chip_at(d), seq),
                    device_id_type=MESH,
                )
                weights[d, index].start()
            for d in range(n_chip):
                held = rows(chip_from(d), shard)
                forwards[d, index] = pltpu.make_async_remote_copy(
                    src_ref=src if d == 0 else dst.at[held],
                    dst_ref=dst.at[held],
                    send_sem=f_send.at[d, index],
                    recv_sem=f_recv.at[d, index],
                    device_id=(sibling, seq),
                    device_id_type=MESH,
                )
            forwards[0, index].start()
    for load in late_loads:
        load.start()
    for load in own_loads:
        load.wait()

    q_gain = q_gain_ref[...].reshape(1, -1)
    k_gain = k_gain_ref[...].reshape(1, -1)
    ones = jnp.ones((total_out.shape[1], txt + img), BF16)
    mix_copies = {}
    for which in range(2):
        for d in range(1, n_seq):
            a2a[d, which].wait_recv()
        mixed = [None] * heads
        total = [None] * heads
        queries = []
        for h in range(heads):
            lanes = slice(h * HEAD, (h + 1) * HEAD)
            parts = [norm_head(q_buf[j, which, :, lanes], q_gain) for j in range(n_seq)]
            queries.append(jnp.concatenate(parts, axis=0))
        for e in range(half):
            if e:
                for index in range(4):
                    a2a[e, which, index].wait_recv()
            for h in range(heads):
                lanes = slice(h * HEAD, (h + 1) * HEAD)
                keys = norm_head(k_buf[e, which, :, lanes], k_gain)
                exponent = jnp.exp(dot_rows(queries[h], keys) * HEAD**-0.5)
                narrow = exponent.astype(BF16)
                if which:
                    part_total = jnp.sum(exponent, axis=-1, keepdims=True)
                else:
                    part_total = dot_rows(ones, narrow)
                part_mixed = dot(narrow, v_buf[e, which, :, lanes])
                total[h] = part_total if e == 0 else total[h] + part_total
                mixed[h] = part_mixed if e == 0 else mixed[h] + part_mixed
        if not which:
            for h in range(heads):
                mix_out[:, h * HEAD : (h + 1) * HEAD] = mixed[h].astype(BF16)
                total_out[h] = total[h]
            for index, (src, dst) in enumerate(((mix_out, mix_in), (total_out, total_in))):
                mix_copies[index] = pltpu.make_async_remote_copy(
                    src_ref=src,
                    dst_ref=dst,
                    send_sem=mix_send.at[index],
                    recv_sem=mix_recv.at[index],
                    device_id=(dp, peer(half)),
                    device_id_type=MESH,
                )
                mix_copies[index].start()
    for index in range(2):
        mix_copies[index].wait_recv()
    for h in range(heads):
        lanes = slice(h * HEAD, (h + 1) * HEAD)
        whole = total[h] + jnp.transpose(total_in[h])[:, 0:1]
        attended_ref[:, lanes] = ((mixed[h] + mix_in[:, lanes].astype(F32)) / whole).astype(BF16)

    image_tokens = attended_ref.shape[0]
    pooled = dot(pool_map((tokens, image_tokens), 1), attended_ref[...])
    pooled_buf[0] = pooled.astype(BF16)

    def spread_to(kind, src_of, dst_of):
        copies = {}
        for d in range(1, n_seq):
            copies[d] = pltpu.make_async_remote_copy(
                src_ref=src_of(d),
                dst_ref=dst_of(d),
                send_sem=x_send.at[kind, d],
                recv_sem=x_recv.at[kind, d],
                device_id=(dp, peer(d)),
                device_id_type=MESH,
            )
            copies[d].start()
        return copies

    pooled_copies = spread_to(0, lambda d: pooled_buf.at[0], lambda d: pooled_buf.at[d])
    for load in late_loads:
        load.wait()
    if gather_here:
        for index in range(2):
            for d in range(1, n_chip):
                weights[d, index].wait_recv()
                forwards[d, index].start()

    residual = pos_ref[...]
    for d in range(n_seq):
        if d:
            pooled_copies[d].wait_recv()
        residual = residual + dot(pooled_buf[d], embed[rows(source(d), width), :])
    resid_in[...] = residual
    normed_in, _ = layer_stats(residual)
    norm_gain = norm_gain_ref[...].reshape(1, -1)
    hidden_in = (normed_in * norm_gain).astype(BF16)
    if gather_here:
        for d in range(n_chip):
            forwards[d, 0].wait_recv()
    activation, derivative = gelu_parts(dot_rows(hidden_in, up_all[...]))
    if gather_here:
        for d in range(n_chip):
            forwards[d, 1].wait_recv()
    part_buf[...] = dot(activation.astype(BF16), down_all[...]).astype(BF16)
    part_copies = spread_to(
        1, lambda d: part_buf.at[rows(peer(d), mine)], lambda d: part_in.at[d]
    )
    own_resid = resid_in[rows(seq, mine), :]
    normed_own, inverse_own = layer_stats(own_resid)
    branch = part_buf[rows(seq, mine), :].astype(F32)
    for d in range(1, n_seq):
        part_copies[d].wait_recv()
        branch = branch + part_in[d].astype(F32)
    normed_out, inverse_out = layer_stats(own_resid + branch)
    direction = (final_gain_ref[...] * direction_ref[...]).reshape(1, -1)
    out_slope = layer_back(direction, normed_out, inverse_out)
    slope_all[rows(seq, mine), :] = out_slope.astype(BF16)
    own_tokens = rows(seq, mine)
    slope_copies = spread_to(
        2, lambda d: slope_all.at[own_tokens], lambda d: slope_all.at[own_tokens]
    )
    score = jnp.sum(jnp.sum(normed_out * direction, axis=-1, keepdims=True), axis=0, keepdims=True)
    score_buf[0] = jnp.broadcast_to(score, score_buf.shape[1:])
    score_copies = {}
    for d in range(1, n_seq):
        score_copies[d] = pltpu.make_async_remote_copy(
            src_ref=score_buf.at[0],
            dst_ref=score_buf.at[d],
            send_sem=s_send.at[d],
            recv_sem=s_recv.at[d],
            device_id=(dp, peer(d)),
            device_id_type=MESH,
        )
        score_copies[d].start()

    for d in range(1, n_seq):
        slope_copies[d].wait_recv()
    back = dot_rows(slope_all[...], down_all[...])
    part2_buf[...] = dot((back * derivative).astype(BF16), up_all[...]).astype(BF16)
    part2_copies = spread_to(
        3, lambda d: part2_buf.at[rows(peer(d), mine)], lambda d: part2_in.at[d]
    )
    slope_in = part2_buf[rows(seq, mine), :].astype(F32)
    for d in range(1, n_seq):
        part2_copies[d].wait_recv()
        slope_in = slope_in + part2_in[d].astype(F32)
    input_slope = out_slope + layer_back(slope_in * norm_gain, normed_own, inverse_own)
    pooled_own = dot_rows(input_slope.astype(BF16), embed[...]).astype(BF16)
    for owner in range(n_seq):
        slope2_out[owner] = pooled_own[:, owner * width : (owner + 1) * width]
    slope2_in[rows(seq, mine), :] = slope2_out[seq]
    slope2_copies = spread_to(
        4, lambda d: slope2_out.at[peer(d)], lambda d: slope2_in.at[own_tokens]
    )
    score_sum = score_buf[0]
    for d in range(1, n_seq):
        score_copies[d].wait_recv()
        score_sum = score_sum + score_buf[d]
    reward_ref[0] = score_sum[0, 0] * (1.0 / tokens)
    for d in range(1, n_seq):
        slope2_copies[d].wait_recv()
    slope_ref[...] = slope2_in[...]

    for group in (
        a2a,
        mix_copies,
        weights,
        forwards,
        pooled_copies,
        part_copies,
        slope_copies,
        score_copies,
        part2_copies,
        slope2_copies,
    ):
        for copy in group.values():
            copy.wait_send()


def on_device(
    n_dp,
    n_seq,
    image_query,
    image_key,
    image_value,
    text_key,
    text_value,
    query_gain,
    key_gain,
    embed_weight,
    position_embed,
    norm_gain,
    final_gain,
    up_weight,
    down_weight,
    reward_direction,
):
    gather_here = n_dp % 2 == 0 and n_dp <= 16 and up_weight.shape[0] % 16 == 0
    if not gather_here:
        up_weight = lax.all_gather(up_weight, "dp", axis=0, tiled=True)
        down_weight = lax.all_gather(down_weight, "dp", axis=0, tiled=True)
    img, txt = image_query.shape[1], text_key.shape[1]
    features, emb = embed_weight.shape
    width = features // n_seq
    tokens = position_embed.shape[0]
    mine = tokens // n_seq
    hidden = up_weight.shape[0] * (n_dp if gather_here else 1)
    n_chip = n_dp // 2 if gather_here else 1
    keys = img + txt
    vmem = pl.BlockSpec(memory_space=pltpu.VMEM)
    dma = pltpu.SemaphoreType.DMA
    attended, slope, reward = pl.pallas_call(
        functools.partial(tower_kernel, n_dp, n_seq, gather_here),
        out_shape=(
            jax.ShapeDtypeStruct((img * n_seq, width), BF16),
            jax.ShapeDtypeStruct((tokens, width), BF16),
            jax.ShapeDtypeStruct((1,), F32),
        ),
        in_specs=[pl.BlockSpec(memory_space=pltpu.HBM)] * 14,
        out_specs=(vmem, vmem, pl.BlockSpec(memory_space=pltpu.SMEM)),
        scratch_shapes=[
            pltpu.VMEM((n_seq, 2, img, width), BF16),
            pltpu.VMEM((n_seq // 2, 2, keys, width), BF16),
            pltpu.VMEM((n_seq // 2, 2, keys, width), BF16),
            pltpu.VMEM((n_seq * img, width), BF16),
            pltpu.VMEM((n_seq * img, width), BF16),
            pltpu.VMEM((width // HEAD, 8, n_seq * img), F32),
            pltpu.VMEM((width // HEAD, 8, n_seq * img), F32),
            pltpu.VMEM((HEAD,), F32),
            pltpu.VMEM((HEAD,), F32),
            pltpu.VMEM((tokens, emb), F32),
            pltpu.VMEM((emb,), F32),
            pltpu.VMEM((emb,), F32),
            pltpu.VMEM((emb,), F32),
            pltpu.VMEM((features, emb), BF16),
            pltpu.VMEM((hidden, emb), BF16),
            pltpu.VMEM((hidden, emb), BF16),
            pltpu.VMEM((n_seq, tokens, width), BF16),
            pltpu.VMEM((tokens, emb), F32),
            pltpu.VMEM((tokens, emb), BF16),
            pltpu.VMEM((n_seq, mine, emb), BF16),
            pltpu.VMEM((tokens, emb), BF16),
            pltpu.VMEM((tokens, emb), BF16),
            pltpu.VMEM((n_seq, mine, emb), BF16),
            pltpu.VMEM((n_seq, mine, width), BF16),
            pltpu.VMEM((tokens, width), BF16),
            pltpu.VMEM((n_seq, 8, 128), F32),
            dma((24,)),
            dma((n_seq, 2)),
            dma((n_seq, 2)),
            dma((n_seq // 2, 2, 4)),
            dma((n_seq // 2, 2, 4)),
            dma((2,)),
            dma((2,)),
            dma((n_chip, 2)),
            dma((n_chip, 2)),
            dma((n_chip, 2)),
            dma((n_chip, 2)),
            dma((5, n_seq)),
            dma((5, n_seq)),
            dma((n_seq,)),
            dma((n_seq,)),
        ],
        compiler_params=pltpu.CompilerParams(
            collective_id=0, has_side_effects=True, vmem_limit_bytes=(64 * 1024 - 256) * 1024
        ),
    )(
        image_query,
        image_key,
        image_value,
        text_key,
        text_value,
        query_gain,
        key_gain,
        embed_weight,
        position_embed,
        norm_gain,
        final_gain,
        up_weight,
        down_weight,
        reward_direction,
    )
    result = jax.ShapeDtypeStruct((img * n_seq, width), BF16)
    attended, gradient = pl.pallas_call(
        finish_kernel,
        out_shape=(result, result),
        in_specs=[vmem, vmem],
        out_specs=(vmem, vmem),
    )(attended, slope)
    return attended[None], gradient[None], reward


def solution(mesh):
    return jax.shard_map(
        functools.partial(on_device, mesh.shape["dp"], mesh.shape["seq"]),
        mesh=mesh,
        in_specs=(
            P("dp", "seq", None),
            P("dp", "seq", None),
            P("dp", "seq", None),
            P("dp", "seq", None),
            P("dp", "seq", None),
            P(),
            P(),
            P(),
            P(),
            P(),
            P(),
            P(("dp", "seq"), None),
            P(("dp", "seq"), None),
            P(),
        ),
        out_specs=(P("dp", None, "seq"), P("dp", None, "seq"), P("dp")),
        check_vma=False,
    )
```
